512 devices in a mesh: dp: 32 (over z, x), mp: 16 (over y, core).
Axes of the slice: x: 4, y: 8, z: 8, core: 2. Of those that a mesh axis runs over, the one named last changes fastest.
Arguments:
- grad: bfloat16 [32, 1, 256, 36864], P('dp', None, None, 'mp'), may hold values from -12 to 12
- error: bfloat16 [32, 1, 256, 36864], P('dp', None, None, 'mp'), may hold values from -6 to 6
- q_init: float32 [1, 36864, 32], P(None, 'mp'), may hold values from -0.03125 to 0.03125
Outputs:
- approx: bfloat16 [1, 256, 36864], P(None, None, 'mp')
- q_new: float32 [1, 36864, 32], P(None, 'mp')
The draws below stay inside these ranges and needn't reach their ends.
All inputs are finite; a program needn't handle non-finite values.
Results may differ from the reference program's by a relative error of at most 0.0083.
Values sent between devices are 32-bit elements; how exact they have to be, the bound alone decides.
No kernel may reach another device: no remote copies, remote signals or barrier semaphores. Data moves between devices by JAX's collectives and lax.ppermute only.
A program may use at most 64 MiB of HBM per device.

```python
import jax
import jax.numpy as jnp
from jax import lax

RANK = 32
ROWS = 256
LAYERS = 1
FF = 36864
REPLICAS = 32
N_DP = 32


def block_scale(stream_key, extent, split, low, top_value):
    def one(dim, parts):
        draws = jax.random.uniform(jax.random.fold_in(jax.random.fold_in(stream_key, 6), dim), (parts,), jnp.float32, low / len(split), top_value / len(split))
        return jnp.repeat(jnp.exp(draws), extent[dim] // parts).reshape((-1,) + (1,) * (len(extent) - dim - 1))

    level = one(*split[0])
    for cut in split[1:]:
        level = level * one(*cut)
    return level


def scatter_about(stream_key, shape, scale, limit, split=(), kind=jnp.bfloat16):
    array = scale * jax.random.normal(stream_key, shape, jnp.float32)
    if split:
        array = array * block_scale(stream_key, shape, split, -0.22, 0.18)
    return jnp.clip(array, -limit, limit).astype(kind)


def setup_inputs(seed: int = 0) -> dict:
    key_of = jax.random.split(jax.random.key(seed), 4)
    grad = scatter_about(key_of[0], (REPLICAS, LAYERS, ROWS, FF), 2.0, 12.0, ((0, 32), (3, 16)))
    error = scatter_about(key_of[1], (REPLICAS, LAYERS, ROWS, FF), 1.0, 6.0, ((0, 32), (3, 16)))
    q_init = scatter_about(key_of[2], (LAYERS, FF, RANK), FF ** -0.5, 0.03125, ((1, 16),), jnp.float32)
    return {"grad": grad, "error": error, "q_init": q_init}


def reference(grad, error, q_init):
    hi = lax.Precision.HIGHEST
    q_low = q_init.astype(jnp.bfloat16).astype(jnp.float32)

    def corrected_of(g_rep, e_rep):
        return (g_rep.astype(jnp.float32) + e_rep.astype(jnp.float32)).astype(jnp.bfloat16).astype(jnp.float32)

    def p_term(carry, pair):
        fixed = corrected_of(pair[0], pair[1])
        return (carry + jnp.einsum('lrf,lfk->lrk', fixed, q_low, precision=hi), None)
    p_zero = jnp.zeros((LAYERS, ROWS, RANK), jnp.float32)
    p_sum, unused = lax.scan(p_term, p_zero, (grad, error))
    gram = jnp.einsum('lrk,lrj->lkj', p_sum, p_sum, precision=hi)
    lower = jnp.linalg.cholesky(gram)

    def solve_one(low, pmat):
        return jax.scipy.linalg.solve_triangular(low, pmat.T, lower=True).T
    basis = jax.vmap(solve_one)(lower, p_sum)
    basis_low = basis.astype(jnp.bfloat16).astype(jnp.float32)

    def q_term(carry, pair):
        fixed = corrected_of(pair[0], pair[1])
        return (carry + jnp.einsum('lrf,lrk->lfk', fixed, basis_low, precision=hi), None)
    q_zero = jnp.zeros((LAYERS, FF, RANK), jnp.float32)
    q_new, unused2 = lax.scan(q_term, q_zero, (grad, error))
    approx = jnp.einsum('lrk,lfk->lrf', basis, q_new, precision=hi) / N_DP
    return (approx.astype(jnp.bfloat16), q_new)
```

```python
import jax
import jax.numpy as jnp
import numpy as np
from jax import lax
from jax.sharding import PartitionSpec as P

HIGHEST = lax.Precision.HIGHEST
BOTH = ("dp", "mp")
SIDES = {"z": 8, "x": 4, "y": 8, "c": 2}


def groups_along(axes):
    names = list(SIDES)
    ids = np.arange(512).reshape(tuple(SIDES.values()))
    inner = [names.index(a) for a in axes]
    outer = [i for i in range(4) if i not in inner]
    size = int(np.prod([ids.shape[i] for i in inner]))
    return np.transpose(ids, outer + inner).reshape(-1, size).tolist()


def sum_along(x, axes):
    groups = groups_along(axes)
    sent = jnp.broadcast_to(x[None], (len(groups[0]),) + x.shape)
    return jnp.sum(lax.all_to_all(sent, BOTH, 0, 0, axis_index_groups=groups), axis=0)


def pieces(x, count):
    out = []
    for _ in range(count):
        top = lax.reduce_precision(x, 8, 7)
        out.append(top.astype(jnp.bfloat16))
        x = x - top
    return out


def dot(a, b, dims, **kw):
    return lax.dot_general(a, b, (dims, ((), ())), preferred_element_type=jnp.float32, **kw)


def local(grad, error, q_init):
    corrected = (grad[0, 0].astype(jnp.float32) + error[0, 0].astype(jnp.float32)).astype(jnp.bfloat16)
    q_low = q_init[0].astype(jnp.bfloat16)
    p = dot(q_low, corrected, ((0,), (1,)))
    for axes in ("xc", "z", "y"):
        p = sum_along(p, axes)
    stacked = dot(jnp.concatenate(pieces(p, 3), axis=0), corrected, ((1,), (0,)))
    raw = stacked[:32] + stacked[32:64] + stacked[64:]
    mine = jnp.sum(lax.all_to_all(raw, "dp", 0, 0, tiled=True), axis=0)
    raw = lax.all_to_all(jnp.broadcast_to(mine[None], raw.shape), "dp", 0, 0, tiled=True)
    gram = dot(p, p, ((1,), (1,)), precision=HIGHEST)
    lower = jnp.linalg.cholesky(gram)
    inverse = jax.scipy.linalg.solve_triangular(lower, jnp.eye(32, dtype=jnp.float32), lower=True)
    basis = dot(inverse, p, ((1,), (0,)), precision=HIGHEST)
    q_new = dot(inverse, raw, ((1,), (0,)), precision=HIGHEST)
    b1, b2 = pieces(basis, 2)
    q1, q2 = pieces(q_new, 2)
    left = jnp.concatenate([b1, b2, b1], axis=0)
    right = jnp.concatenate([q1, q1, q2], axis=0)
    approx = dot(left, right, ((0,), (0,))) / lax.axis_size("dp")
    return (approx.astype(jnp.bfloat16)[None], q_new.T[None])


def solution(mesh):
    placed = (P("dp", None, None, "mp"), P("dp", None, None, "mp"), P(None, "mp", None))
    return jax.shard_map(
        local,
        mesh=mesh,
        in_specs=placed,
        out_specs=(P(None, None, "mp"), P(None, "mp", None)),
        check_vma=False,
    )
```

```python
import jax
import jax.numpy as jnp
import numpy as np
from jax import lax
from jax.sharding import PartitionSpec as P

HIGHEST = lax.Precision.HIGHEST
BOTH = ("dp", "mp")
BITS = ("z2", "z1", "z0", "x1", "x0", "y2", "y1", "y0", "c")
NEAR = ("x1", "x0", "y0", "c")
FAR = ("z2", "z1", "z0", "y2", "y1")


def groups_along(bits):
    ids = np.arange(512).reshape((2,) * 9)
    inner = [i for i, b in enumerate(BITS) if b in bits]
    outer = [i for i, b in enumerate(BITS) if b not in bits]
    return np.transpose(ids, outer + inner).reshape(-1, 2 ** len(inner)).tolist()


def exchange(x, bits):
    return lax.all_to_all(x, BOTH, 0, 0, axis_index_groups=groups_along(bits))


def spread(x, count):
    return jnp.broadcast_to(x[None], (count,) + x.shape)


def sum_all(p):
    part = jnp.sum(exchange(p.reshape(16, p.shape[0] // 16, p.shape[1]), NEAR), axis=0)
    part = jnp.sum(exchange(spread(part, 32), FAR), axis=0)
    return exchange(spread(part, 16), NEAR).reshape(p.shape)


def pieces(x, count):
    out = []
    for _ in range(count):
        top = lax.reduce_precision(x, 8, 7)
        out.append(top.astype(jnp.bfloat16))
        x = x - top
    return out


def dot(a, b, dims, **kw):
    return lax.dot_general(a, b, (dims, ((), ())), preferred_element_type=jnp.float32, **kw)


def local(grad, error, q_init):
    corrected = (grad[0, 0].astype(jnp.float32) + error[0, 0].astype(jnp.float32)).astype(jnp.bfloat16)
    q_low = q_init[0].astype(jnp.bfloat16)
    p = dot(q_low, corrected, ((0,), (1,)))
    p = sum_all(p)
    stacked = dot(jnp.concatenate(pieces(p, 3), axis=0), corrected, ((1,), (0,)))
    raw = stacked[:32] + stacked[32:64] + stacked[64:]
    mine = jnp.sum(lax.all_to_all(raw, "dp", 0, 0, tiled=True), axis=0)
    raw = lax.all_to_all(jnp.broadcast_to(mine[None], raw.shape), "dp", 0, 0, tiled=True)
    gram = dot(p, p, ((1,), (1,)), precision=HIGHEST)
    lower = jnp.linalg.cholesky(gram)
    inverse = jax.scipy.linalg.solve_triangular(lower, jnp.eye(32, dtype=jnp.float32), lower=True)
    basis = dot(inverse, p, ((1,), (0,)), precision=HIGHEST)
    q_new = dot(inverse, raw, ((1,), (0,)), precision=HIGHEST)
    b1, b2 = pieces(basis, 2)
    q1, q2 = pieces(q_new, 2)
    left = jnp.concatenate([b1, b2, b1], axis=0)
    right = jnp.concatenate([q1, q1, q2], axis=0)
    approx = dot(left, right, ((0,), (0,))) / lax.axis_size("dp")
    return (approx.astype(jnp.bfloat16)[None], q_new.T[None])


def solution(mesh):
    placed = (P("dp", None, None, "mp"), P("dp", None, None, "mp"), P(None, "mp", None))
    return jax.shard_map(
        local,
        mesh=mesh,
        in_specs=placed,
        out_specs=(P(None, None, "mp"), P(None, "mp", None)),
        check_vma=False,
    )
```

```python
import jax
import jax.numpy as jnp
import numpy as np
from jax import lax
from jax.experimental import pallas as pl
from jax.experimental.pallas import tpu as pltpu
from jax.sharding import PartitionSpec as P

HIGHEST = lax.Precision.HIGHEST
BOTH = ("dp", "mp")
BITS = ("z2", "z1", "z0", "x1", "x0", "y2", "y1", "y0", "c")
NEAR = ("x1", "x0", "y0", "c")
FAR = ("z2", "z1", "z0", "y2", "y1")
ROWS, RANK, COLS, PEERS = 256, 32, 2304, 32
LANES = 128
TILES = COLS // LANES
WIDE = 768
LIMIT = 12 * 1024 * 1024
F32, BF16 = jnp.float32, jnp.bfloat16


def groups_along(bits):
    ids = np.arange(512).reshape((2,) * 9)
    inner = [i for i, b in enumerate(BITS) if b in bits]
    outer = [i for i, b in enumerate(BITS) if b not in bits]
    return np.transpose(ids, outer + inner).reshape(-1, 2 ** len(inner)).tolist()


def exchange(x, bits):
    return lax.all_to_all(x, BOTH, 0, 0, axis_index_groups=groups_along(bits))


def spread(x, count):
    return jnp.broadcast_to(x[None], (count,) + x.shape)


def sum_all(p):
    part = jnp.sum(exchange(p.reshape(16, p.shape[0] // 16, p.shape[1]), NEAR), axis=0)
    part = jnp.sum(exchange(spread(part, 32), FAR), axis=0)
    return exchange(spread(part, 16), NEAR).reshape(p.shape)


def cut(x, count):
    out = []
    for _ in range(count):
        top = x.astype(BF16)
        out.append(top)
        x = x - top.astype(F32)
    return out


def pieces(x, count):
    out = []
    for _ in range(count):
        top = lax.reduce_precision(x, 8, 7)
        out.append(top.astype(BF16))
        x = x - top
    return out


def dot(a, b, dims, **kw):
    return lax.dot_general(a, b, (dims, ((), ())), preferred_element_type=F32, **kw)


def project(grad, error, q_init, p_out, corrected, g, e, q, sems):
    def copies(i):
        cols = pl.ds(i * WIDE, WIDE)
        return [
            pltpu.make_async_copy(src.at[:, cols], dst.at[:, cols], sems.at[i, j])
            for j, (src, dst) in enumerate(((grad, g), (error, e), (q_init, q)))
        ]

    for i in range(COLS // WIDE):
        for copy in copies(i):
            copy.start()
    total = jnp.zeros((RANK, ROWS), F32)
    for i in range(COLS // WIDE):
        for copy in copies(i):
            copy.wait()
        cols = pl.ds(i * WIDE, WIDE)
        both = (g[:, cols].astype(F32) + e[:, cols].astype(F32)).astype(BF16)
        corrected[:, cols] = both
        total = total + dot(q[:, cols].astype(BF16), both, ((1,), (1,)))
    p_out[...] = total


def partial(p, corrected, out):
    left = jnp.concatenate(cut(p[...], 3), axis=0)
    for t in range(0, TILES, 2):
        acc = dot(left, corrected[:, pl.ds(t * LANES, 2 * LANES)], ((1,), (0,)))
        acc = acc[:RANK] + acc[RANK : 2 * RANK] + acc[2 * RANK :]
        for h in range(2):
            for k in range(0, RANK, 8):
                out[pl.ds(k * TILES + t + h, 8, stride=TILES), :] = acc[k : k + 8, h * LANES : (h + 1) * LANES]


def gathered(x, out):
    for t in range(TILES):
        at = [pl.ds(k * TILES + t, 8, stride=TILES) for k in range(0, PEERS, 8)]
        acc = (x[at[0], :] + x[at[1], :]) + (x[at[2], :] + x[at[3], :])
        acc = jnp.broadcast_to(jnp.sum(acc, axis=0, keepdims=True), (8, LANES))
        for rows in at:
            out[rows, :] = acc


def finish(raw, inverse, basis, approx_out, q_out, approx, q_new, sems):
    pending = []
    for i in range(COLS // WIDE):
        parts = []
        for t in range(i * WIDE // LANES, (i + 1) * WIDE // LANES):
            rows = [raw[pl.ds(k * TILES + t, 8, stride=TILES), :] for k in range(0, RANK, 8)]
            parts.append(jnp.concatenate(rows, axis=0))
        r1, r2, r3 = cut(jnp.concatenate(parts, axis=1), 3)
        q = dot(inverse[...], jnp.concatenate([r1, r2, r1, r2, r3, r1], axis=0), ((1,), (0,)))
        cols = pl.ds(i * WIDE, WIDE)
        q_new[:, cols] = q
        q1, q2 = cut(q, 2)
        approx[:, cols] = dot(basis[...], jnp.concatenate([q1, q1, q2], axis=0), ((1,), (0,))).astype(BF16)
        for j, (src, dst) in enumerate(((approx, approx_out), (q_new, q_out))):
            copy = pltpu.make_async_copy(src.at[:, cols], dst.at[:, cols], sems.at[i, j])
            copy.start()
            pending.append(copy)
    for copy in pending:
        copy.wait()


def in_vmem(x):
    return pltpu.with_memory_space_constraint(x, pltpu.VMEM)


def in_hbm(x):
    return pltpu.with_memory_space_constraint(x, pltpu.HBM)


PARAMS = pltpu.CompilerParams(vmem_limit_bytes=LIMIT)
VMEM, HBM = pl.BlockSpec(memory_space=pltpu.VMEM), pl.BlockSpec(memory_space=pltpu.HBM)
CHUNKS = COLS // WIDE
LINEAR = (RANK * TILES, LANES)


def local(grad, error, q_init):
    p, corrected = pl.pallas_call(
        project,
        out_shape=(pltpu.VMEM((RANK, ROWS), F32), pltpu.VMEM((ROWS, COLS), BF16)),
        in_specs=[HBM] * 3,
        out_specs=(VMEM, VMEM),
        scratch_shapes=[
            pltpu.VMEM((ROWS, COLS), BF16),
            pltpu.VMEM((ROWS, COLS), BF16),
            pltpu.VMEM((RANK, COLS), F32),
            pltpu.SemaphoreType.DMA((CHUNKS, 3)),
        ],
        compiler_params=PARAMS,
        name="project",
    )(in_hbm(grad[0, 0]), in_hbm(error[0, 0]), in_hbm(q_init[0].T))
    p = sum_all(p)
    raw = pl.pallas_call(
        partial,
        out_shape=pltpu.VMEM(LINEAR, F32),
        in_specs=[VMEM] * 2,
        out_specs=VMEM,
        compiler_params=PARAMS,
        name="partial",
    )(in_vmem(p), in_vmem(corrected))
    raw = lax.all_to_all(raw.reshape(PEERS, 1, COLS), "dp", 0, 0, tiled=True)
    raw = pl.pallas_call(
        gathered,
        out_shape=pltpu.VMEM(LINEAR, F32),
        in_specs=[VMEM],
        out_specs=VMEM,
        compiler_params=PARAMS,
        name="gathered",
    )(in_vmem(raw.reshape(LINEAR)))
    raw = lax.all_to_all(raw.reshape(PEERS, 1, COLS), "dp", 0, 0, tiled=True).reshape(LINEAR)
    gram = dot(p, p, ((1,), (1,)), precision=HIGHEST)
    lower = jnp.linalg.cholesky(gram)
    inverse = jax.scipy.linalg.solve_triangular(lower, jnp.eye(RANK, dtype=F32), lower=True)
    basis = dot(p, inverse, ((0,), (1,)), precision=HIGHEST) / lax.axis_size("dp")
    b1, b2 = pieces(basis, 2)
    i1, i2, i3 = pieces(inverse, 3)
    approx, q_new = pl.pallas_call(
        finish,
        out_shape=(jax.ShapeDtypeStruct((ROWS, COLS), BF16), jax.ShapeDtypeStruct((RANK, COLS), F32)),
        in_specs=[VMEM] * 3,
        out_specs=(HBM, HBM),
        scratch_shapes=[
            pltpu.VMEM((ROWS, COLS), BF16),
            pltpu.VMEM((RANK, COLS), F32),
            pltpu.SemaphoreType.DMA((CHUNKS, 2)),
        ],
        compiler_params=PARAMS,
        name="finish",
    )(
        in_vmem(raw),
        in_vmem(jnp.concatenate([i1, i1, i2, i2, i1, i3], axis=1)),
        in_vmem(jnp.concatenate([b1, b2, b1], axis=1)),
    )
    return (approx[None], q_new.T[None])


def solution(mesh):
    placed = (P("dp", None, None, "mp"), P("dp", None, None, "mp"), P(None, "mp", None))
    return jax.shard_map(
        local,
        mesh=mesh,
        in_specs=placed,
        out_specs=(P(None, None, "mp"), P(None, "mp", None)),
        check_vma=False,
    )
```

```python
import jax
import jax.numpy as jnp
import numpy as np
from jax import lax
from jax.experimental import pallas as pl
from jax.experimental.pallas import tpu as pltpu
from jax.sharding import PartitionSpec as P

HIGHEST = lax.Precision.HIGHEST
BOTH = ("dp", "mp")
BITS = ("z2", "z1", "z0", "x1", "x0", "y2", "y1", "y0", "c")
NEAR = ("x1", "x0", "y0", "c")
FAR = ("z2", "z1", "z0", "y2", "y1")
ALONG_DP = ("z2", "z1", "z0", "x1", "x0")
FIRST_P = ("z2", "z1", "x1", "y2", "y0", "c")
FIRST_Q = ("z2", "x1")
ROWS, RANK, COLS, PEERS = 256, 32, 2304, 32
LANES = 128
TILES = COLS // LANES
WIDE = 768
LIMIT = 12 * 1024 * 1024
F32, BF16 = jnp.float32, jnp.bfloat16


def groups_along(bits, first):
    ids = np.arange(512).reshape((2,) * 9)
    inner = [i for i, b in enumerate(BITS) if b in bits]
    outer = [i for i, b in enumerate(BITS) if b not in bits]
    groups = np.transpose(ids, outer + inner).reshape(-1, 2 ** len(inner))
    start = sum(1 << (len(BITS) - 1 - i) for i in inner if BITS[i] in first)
    return (groups ^ start).tolist()


def exchange(x, bits, first):
    return lax.all_to_all(x, BOTH, 0, 0, axis_index_groups=groups_along(bits, first))


def spread(x, count):
    return jnp.broadcast_to(x[None], (count,) + x.shape)


def sum_all(p):
    near, far = 2 ** len(NEAR), 2 ** len(FAR)
    part = jnp.sum(exchange(p.reshape(near, p.shape[0] // near, p.shape[1]), NEAR, FIRST_P), axis=0)
    part = jnp.sum(exchange(spread(part, far), FAR, FIRST_P), axis=0)
    return exchange(spread(part, near), NEAR, FIRST_P).reshape(p.shape)


def cut(x, count):
    out = []
    for _ in range(count):
        top = x.astype(BF16)
        out.append(top)
        x = x - top.astype(F32)
    return out


def pieces(x, count):
    out = []
    for _ in range(count):
        top = lax.reduce_precision(x, 8, 7)
        out.append(top.astype(BF16))
        x = x - top
    return out


def dot(a, b, dims, **kw):
    return lax.dot_general(a, b, (dims, ((), ())), preferred_element_type=F32, **kw)


def project(grad, error, q_init, p_out, corrected, g, e, q, sems):
    def copies(i):
        cols = pl.ds(i * WIDE, WIDE)
        return [
            pltpu.make_async_copy(src.at[:, cols], dst.at[:, cols], sems.at[i, j])
            for j, (src, dst) in enumerate(((grad, g), (error, e), (q_init, q)))
        ]

    for i in range(COLS // WIDE):
        for copy in copies(i):
            copy.start()
    total = jnp.zeros((RANK, ROWS), F32)
    for i in range(COLS // WIDE):
        for copy in copies(i):
            copy.wait()
        cols = pl.ds(i * WIDE, WIDE)
        both = (g[:, cols].astype(F32) + e[:, cols].astype(F32)).astype(BF16)
        corrected[:, cols] = both
        total = total + dot(q[:, cols].astype(BF16), both, ((1,), (1,)))
    p_out[...] = total


def tile_rows(k, t):
    return pl.ds(8 * (k * TILES + t), 8)


def partial(p, corrected, out):
    left = jnp.concatenate(cut(p[...], 3), axis=0)
    for t in range(0, TILES, 2):
        acc = dot(left, corrected[:, pl.ds(t * LANES, 2 * LANES)], ((1,), (0,)))
        acc = acc[:RANK] + acc[RANK : 2 * RANK] + acc[2 * RANK :]
        for h in range(2):
            for k in range(RANK // 8):
                out[tile_rows(k, t + h), :] = acc[8 * k : 8 * k + 8, h * LANES : (h + 1) * LANES]


def gathered(x, out):
    size = 4 * TILES
    acc = x[pl.ds(0, size), :]
    for i in range(1, PEERS // 4):
        acc = acc + x[pl.ds(i * size, size), :]
    one = (acc[:TILES] + acc[TILES : 2 * TILES]) + (acc[2 * TILES : 3 * TILES] + acc[3 * TILES :])
    four = jnp.concatenate([one] * 4, axis=0)
    for i in range(PEERS // 4):
        out[pl.ds(i * size, size), :] = four


def finish(raw, inverse, basis, approx_out, q_out, approx, q_new, sems):
    pending = []
    for i in range(COLS // WIDE):
        parts = []
        for t in range(i * WIDE // LANES, (i + 1) * WIDE // LANES):
            parts.append(jnp.concatenate([raw[tile_rows(k, t), :] for k in range(RANK // 8)], axis=0))
        r1, r2, r3 = cut(jnp.concatenate(parts, axis=1), 3)
        q = dot(inverse[...], jnp.concatenate([r1, r2, r1, r2, r3, r1], axis=0), ((1,), (0,)))
        cols = pl.ds(i * WIDE, WIDE)
        q_new[:, cols] = q
        q1, q2 = cut(q, 2)
        approx[:, cols] = dot(basis[...], jnp.concatenate([q1, q1, q2], axis=0), ((1,), (0,))).astype(BF16)
        for j, (src, dst) in enumerate(((approx, approx_out), (q_new, q_out))):
            copy = pltpu.make_async_copy(src.at[:, cols], dst.at[:, cols], sems.at[i, j])
            copy.start()
            pending.append(copy)
    for copy in pending:
        copy.wait()


def in_vmem(x):
    return pltpu.with_memory_space_constraint(x, pltpu.VMEM)


def in_hbm(x):
    return pltpu.with_memory_space_constraint(x, pltpu.HBM)


PARAMS = pltpu.CompilerParams(vmem_limit_bytes=LIMIT)
VMEM, HBM = pl.BlockSpec(memory_space=pltpu.VMEM), pl.BlockSpec(memory_space=pltpu.HBM)
CHUNKS = COLS // WIDE
LINEAR = (RANK * TILES, LANES)


def local(grad, error, q_init):
    p, corrected = pl.pallas_call(
        project,
        out_shape=(pltpu.VMEM((RANK, ROWS), F32), pltpu.VMEM((ROWS, COLS), BF16)),
        in_specs=[HBM] * 3,
        out_specs=(VMEM, VMEM),
        scratch_shapes=[
            pltpu.VMEM((ROWS, COLS), BF16),
            pltpu.VMEM((ROWS, COLS), BF16),
            pltpu.VMEM((RANK, COLS), F32),
            pltpu.SemaphoreType.DMA((CHUNKS, 3)),
        ],
        compiler_params=PARAMS,
        name="project",
    )(in_hbm(grad[0, 0]), in_hbm(error[0, 0]), in_hbm(q_init[0].T))
    p = sum_all(p)
    raw = pl.pallas_call(
        partial,
        out_shape=pltpu.VMEM(LINEAR, F32),
        in_specs=[VMEM] * 2,
        out_specs=VMEM,
        compiler_params=PARAMS,
        name="partial",
    )(in_vmem(p), in_vmem(corrected))
    raw = exchange(raw.reshape(PEERS, 1, COLS), ALONG_DP, FIRST_Q)
    raw = pl.pallas_call(
        gathered,
        out_shape=pltpu.VMEM(LINEAR, F32),
        in_specs=[VMEM],
        out_specs=VMEM,
        compiler_params=PARAMS,
        name="gathered",
    )(in_vmem(raw.reshape(LINEAR)))
    raw = exchange(raw.reshape(PEERS, 1, COLS), ALONG_DP, FIRST_Q).reshape(LINEAR)
    gram = dot(p, p, ((1,), (1,)), precision=HIGHEST)
    lower = jnp.linalg.cholesky(gram)
    inverse = jax.scipy.linalg.solve_triangular(lower, jnp.eye(RANK, dtype=F32), lower=True)
    basis = dot(p, inverse, ((0,), (1,)), precision=HIGHEST) / lax.axis_size("dp")
    b1, b2 = pieces(basis, 2)
    i1, i2, i3 = pieces(inverse, 3)
    approx, q_new = pl.pallas_call(
        finish,
        out_shape=(jax.ShapeDtypeStruct((ROWS, COLS), BF16), jax.ShapeDtypeStruct((RANK, COLS), F32)),
        in_specs=[VMEM] * 3,
        out_specs=(HBM, HBM),
        scratch_shapes=[
            pltpu.VMEM((ROWS, COLS), BF16),
            pltpu.VMEM((RANK, COLS), F32),
            pltpu.SemaphoreType.DMA((CHUNKS, 2)),
        ],
        compiler_params=PARAMS,
        name="finish",
    )(
        in_vmem(raw),
        in_vmem(jnp.concatenate([i1, i1, i2, i2, i1, i3], axis=1)),
        in_vmem(jnp.concatenate([b1, b2, b1], axis=1)),
    )
    return (approx[None], q_new.T[None])


def solution(mesh):
    placed = (P("dp", None, None, "mp"), P("dp", None, None, "mp"), P(None, "mp", None))
    return jax.shard_map(
        local,
        mesh=mesh,
        in_specs=placed,
        out_specs=(P(None, None, "mp"), P(None, "mp", None)),
        check_vma=False,
    )
```

```python
import jax
import jax.numpy as jnp
import numpy as np
from jax import lax
from jax.experimental import pallas as pl
from jax.experimental.pallas import tpu as pltpu
from jax.sharding import PartitionSpec as P

HIGHEST = lax.Precision.HIGHEST
BOTH = ("dp", "mp")
BITS = ("z2", "z1", "z0", "x1", "x0", "y2", "y1", "y0", "c")
NEAR = ("x1", "x0", "y0", "c")
FAR = ("z2", "z1", "z0", "y2", "y1")
ALONG_DP = ("z2", "z1", "z0", "x1", "x0")
FIRST_P = ("z2", "z1", "x1", "y2", "y0", "c")
FIRST_Q = ("z2", "x1")
ROWS, RANK, COLS, PEERS, N_DP = 256, 32, 2304, 32, 32
LANES = 128
TILES = COLS // LANES
WIDE = 768
LIMIT = 12 * 1024 * 1024
F32, BF16 = jnp.float32, jnp.bfloat16


def groups_along(bits, first):
    ids = np.arange(512).reshape((2,) * 9)
    inner = [i for i, b in enumerate(BITS) if b in bits]
    outer = [i for i, b in enumerate(BITS) if b not in bits]
    groups = np.transpose(ids, outer + inner).reshape(-1, 2 ** len(inner))
    start = sum(1 << (len(BITS) - 1 - i) for i in inner if BITS[i] in first)
    return (groups ^ start).tolist()


def exchange(x, bits, first):
    return lax.all_to_all(x, BOTH, 0, 0, axis_index_groups=groups_along(bits, first))


def spread(x, count):
    return jnp.broadcast_to(x[None], (count,) + x.shape)


def sum_all(p):
    near, far = 2 ** len(NEAR), 2 ** len(FAR)
    part = jnp.sum(exchange(p.reshape(near, p.shape[0] // near, p.shape[1]), NEAR, FIRST_P), axis=0)
    part = jnp.sum(exchange(spread(part, far), FAR, FIRST_P), axis=0)
    return exchange(spread(part, near), NEAR, FIRST_P).reshape(p.shape)


def cut(x, count):
    out = []
    for _ in range(count):
        top = x.astype(BF16)
        out.append(top)
        x = x - top.astype(F32)
    return out


def dot(a, b, dims, **kw):
    return lax.dot_general(a, b, (dims, ((), ())), preferred_element_type=F32, **kw)


def project(grad, error, q_init, p_out, corrected, g, e, q, sems):
    def copies(i):
        cols = pl.ds(i * WIDE, WIDE)
        return [
            pltpu.make_async_copy(src.at[:, cols], dst.at[:, cols], sems.at[i, j])
            for j, (src, dst) in enumerate(((grad, g), (error, e), (q_init, q)))
        ]

    for i in range(COLS // WIDE):
        for copy in copies(i):
            copy.start()
    total = jnp.zeros((RANK, ROWS), F32)
    for i in range(COLS // WIDE):
        for copy in copies(i):
            copy.wait()
        cols = pl.ds(i * WIDE, WIDE)
        both = (g[:, cols].astype(F32) + e[:, cols].astype(F32)).astype(BF16)
        corrected[:, cols] = both
        total = total + dot(q[:, cols].astype(BF16), both, ((1,), (1,)))
    p_out[...] = total


def tile_rows(k, t):
    return pl.ds(8 * (k * TILES + t), 8)


def partial(p, corrected, out):
    left = jnp.concatenate(cut(p[...], 3), axis=0)
    for t in range(0, TILES, 2):
        acc = dot(left, corrected[:, pl.ds(t * LANES, 2 * LANES)], ((1,), (0,)))
        acc = acc[:RANK] + acc[RANK : 2 * RANK] + acc[2 * RANK :]
        for h in range(2):
            for k in range(RANK // 8):
                out[tile_rows(k, t + h), :] = acc[8 * k : 8 * k + 8, h * LANES : (h + 1) * LANES]


def factor(p, left):
    p = p[...]
    row = lax.broadcasted_iota(jnp.int32, (RANK, 2 * RANK), 0)
    lane = lax.broadcasted_iota(jnp.int32, (RANK, 2 * RANK), 1)
    unit = jnp.where(lane == row + RANK, 1.0, 0.0)
    gram = dot(p, p, ((1,), (1,)), precision=HIGHEST)
    m = jnp.concatenate([gram, unit[:, RANK:]], axis=1)
    for k in range(RANK - 1):
        ratio = m[:, k : k + 1] / m[k : k + 1, k : k + 1]
        m = m - jnp.where(row > k, ratio, 0.0) * m[k : k + 1, :]
    pivot = jnp.sum(jnp.where(lane == row, m, 0.0), axis=1, keepdims=True)
    inverse = m[:, RANK:] / jnp.sqrt(pivot)
    basis = dot(inverse, p, ((1,), (0,)), precision=HIGHEST)
    weight = dot(inverse.T, basis, ((1,), (0,)), precision=HIGHEST) * (1.0 / N_DP)
    t1, t2, t3 = cut(jnp.concatenate([weight.T, inverse], axis=0), 3)
    left[...] = jnp.concatenate([t1, t1, t2, t2, t1, t3], axis=1)


def gathered(x, out):
    size = 4 * TILES
    acc = x[pl.ds(0, size), :]
    for i in range(1, PEERS // 4):
        acc = acc + x[pl.ds(i * size, size), :]
    one = (acc[:TILES] + acc[TILES : 2 * TILES]) + (acc[2 * TILES : 3 * TILES] + acc[3 * TILES :])
    four = jnp.concatenate([one] * 4, axis=0)
    for i in range(PEERS // 4):
        out[pl.ds(i * size, size), :] = four


def finish(raw, left, approx_out, q_out, approx, q_new, sems):
    pending = []
    for i in range(CHUNKS):
        parts = []
        for t in range(i * WIDE // LANES, (i + 1) * WIDE // LANES):
            parts.append(jnp.concatenate([raw[tile_rows(k, t), :] for k in range(RANK // 8)], axis=0))
        r1, r2, r3 = cut(jnp.concatenate(parts, axis=1), 3)
        both = dot(left[...], jnp.concatenate([r1, r2, r1, r2, r3, r1], axis=0), ((1,), (0,)))
        cols = pl.ds(i * WIDE, WIDE)
        approx[:, cols] = both[:ROWS].astype(BF16)
        q_new[:, cols] = both[ROWS:]
        for j, (src, dst) in enumerate(((approx, approx_out), (q_new, q_out))):
            copy = pltpu.make_async_copy(src.at[:, cols], dst.at[:, cols], sems.at[i, j])
            copy.start()
            pending.append(copy)
    for copy in pending:
        copy.wait()


def in_vmem(x):
    return pltpu.with_memory_space_constraint(x, pltpu.VMEM)


def in_hbm(x):
    return pltpu.with_memory_space_constraint(x, pltpu.HBM)


PARAMS = pltpu.CompilerParams(vmem_limit_bytes=LIMIT)
VMEM, HBM = pl.BlockSpec(memory_space=pltpu.VMEM), pl.BlockSpec(memory_space=pltpu.HBM)
CHUNKS = COLS // WIDE
LINEAR = (RANK * TILES, LANES)


def local(grad, error, q_init):
    p, corrected = pl.pallas_call(
        project,
        out_shape=(pltpu.VMEM((RANK, ROWS), F32), pltpu.VMEM((ROWS, COLS), BF16)),
        in_specs=[HBM] * 3,
        out_specs=(VMEM, VMEM),
        scratch_shapes=[
            pltpu.VMEM((ROWS, COLS), BF16),
            pltpu.VMEM((ROWS, COLS), BF16),
            pltpu.VMEM((RANK, COLS), F32),
            pltpu.SemaphoreType.DMA((CHUNKS, 3)),
        ],
        compiler_params=PARAMS,
        name="project",
    )(in_hbm(grad[0, 0]), in_hbm(error[0, 0]), in_hbm(q_init[0].T))
    p = sum_all(p)
    raw = pl.pallas_call(
        partial,
        out_shape=pltpu.VMEM(LINEAR, F32),
        in_specs=[VMEM] * 2,
        out_specs=VMEM,
        compiler_params=PARAMS,
        name="partial",
    )(in_vmem(p), in_vmem(corrected))
    raw = exchange(raw.reshape(PEERS, 1, COLS), ALONG_DP, FIRST_Q)
    left = pl.pallas_call(
        factor,
        out_shape=pltpu.VMEM((ROWS + RANK, 6 * RANK), BF16),
        in_specs=[VMEM],
        out_specs=VMEM,
        compiler_params=PARAMS,
        cost_estimate=pl.CostEstimate(flops=4_000_000_000, bytes_accessed=0, transcendentals=0),
        name="factor",
    )(in_vmem(p))
    raw, left = lax.optimization_barrier((raw, left))
    raw = pl.pallas_call(
        gathered,
        out_shape=pltpu.VMEM(LINEAR, F32),
        in_specs=[VMEM],
        out_specs=VMEM,
        compiler_params=PARAMS,
        name="gathered",
    )(in_vmem(raw.reshape(LINEAR)))
    raw = exchange(raw.reshape(PEERS, 1, COLS), ALONG_DP, FIRST_Q).reshape(LINEAR)
    approx, q_new = pl.pallas_call(
        finish,
        out_shape=(jax.ShapeDtypeStruct((ROWS, COLS), BF16), jax.ShapeDtypeStruct((RANK, COLS), F32)),
        in_specs=[VMEM] * 2,
        out_specs=(HBM, HBM),
        scratch_shapes=[
            pltpu.VMEM((ROWS, COLS), BF16),
            pltpu.VMEM((RANK, COLS), F32),
            pltpu.SemaphoreType.DMA((CHUNKS, 2)),
        ],
        compiler_params=PARAMS,
        name="finish",
    )(in_vmem(raw), in_vmem(left))
    return (approx[None], q_new.T[None])


def solution(mesh):
    placed = (P("dp", None, None, "mp"), P("dp", None, None, "mp"), P(None, "mp", None))
    return jax.shard_map(
        local,
        mesh=mesh,
        in_specs=placed,
        out_specs=(P(None, None, "mp"), P(None, "mp", None)),
        check_vma=False,
    )
```

```python
import jax
import jax.numpy as jnp
import numpy as np
from jax import lax
from jax.experimental import pallas as pl
from jax.experimental.pallas import tpu as pltpu
from jax.sharding import PartitionSpec as P

HIGHEST = lax.Precision.HIGHEST
BOTH = ("dp", "mp")
BITS = ("z2", "z1", "z0", "x1", "x0", "y2", "y1", "y0", "c")
NEAR = ("x1", "x0", "y0", "c")
FAR = ("z2", "z1", "z0", "y2", "y1")
ALONG_DP = ("z2", "z1", "z0", "x1", "x0")
FIRST_P = ("z2", "z1", "x1", "y2", "y0", "c")
FIRST_Q = ("z2", "x1")
ROWS, RANK, COLS, PEERS, N_DP = 256, 32, 2304, 32, 32
LANES = 128
TILES = COLS // LANES
WIDE = 768
LIMIT = 12 * 1024 * 1024
F32, BF16 = jnp.float32, jnp.bfloat16


def places():
    i = np.arange(512)
    return np.stack([i // 64, i // 16 % 4, i // 2 % 8, i % 2], axis=1)


def groups_along(bits, first):
    ids = np.arange(512).reshape((2,) * 9)
    inner = [i for i, b in enumerate(BITS) if b in bits]
    outer = [i for i, b in enumerate(BITS) if b not in bits]
    groups = np.transpose(ids, outer + inner).reshape(-1, 2 ** len(inner))
    start = sum(1 << (len(BITS) - 1 - i) for i in inner if BITS[i] in first)
    at, size = places(), np.array([8, 4, 8, 2])
    listed = []
    for group in groups:
        root = group[0] ^ start
        apart = np.abs(at[group] - at[root])
        hops = np.minimum(apart, size - apart) @ np.array([4, 4, 4, 1])
        order = np.argsort(-hops, kind="stable")
        rest = [int(m) for m in group[order] if m != root]
        listed.append([int(root)] + rest)
    return listed


def exchange(x, bits, first):
    return lax.all_to_all(x, BOTH, 0, 0, axis_index_groups=groups_along(bits, first))


def spread(x, count):
    return jnp.broadcast_to(x[None], (count,) + x.shape)


def sum_all(p):
    near, far = 2 ** len(NEAR), 2 ** len(FAR)
    part = jnp.sum(exchange(p.reshape(near, p.shape[0] // near, p.shape[1]), NEAR, FIRST_P), axis=0)
    part = jnp.sum(exchange(spread(part, far), FAR, FIRST_P), axis=0)
    return exchange(spread(part, near), NEAR, FIRST_P).reshape(p.shape)


def cut(x, count):
    out = []
    for _ in range(count):
        top = x.astype(BF16)
        out.append(top)
        x = x - top.astype(F32)
    return out


def dot(a, b, dims, **kw):
    return lax.dot_general(a, b, (dims, ((), ())), preferred_element_type=F32, **kw)


def project(grad, error, q_init, p_out, corrected, g, e, q, sems):
    def copies(i):
        cols = pl.ds(i * WIDE, WIDE)
        return [
            pltpu.make_async_copy(src.at[:, cols], dst.at[:, cols], sems.at[i, j])
            for j, (src, dst) in enumerate(((grad, g), (error, e), (q_init, q)))
        ]

    for i in range(COLS // WIDE):
        for copy in copies(i):
            copy.start()
    total = jnp.zeros((RANK, ROWS), F32)
    for i in range(COLS // WIDE):
        for copy in copies(i):
            copy.wait()
        cols = pl.ds(i * WIDE, WIDE)
        both = (g[:, cols].astype(F32) + e[:, cols].astype(F32)).astype(BF16)
        corrected[:, cols] = both
        total = total + dot(q[:, cols].astype(BF16), both, ((1,), (1,)))
    p_out[...] = total


def tile_rows(k, t):
    return pl.ds(8 * (k * TILES + t), 8)


def partial(p, corrected, out):
    left = jnp.concatenate(cut(p[...], 3), axis=0)
    for t in range(0, TILES, 2):
        acc = dot(left, corrected[:, pl.ds(t * LANES, 2 * LANES)], ((1,), (0,)))
        acc = acc[:RANK] + acc[RANK : 2 * RANK] + acc[2 * RANK :]
        for h in range(2):
            for k in range(RANK // 8):
                out[tile_rows(k, t + h), :] = acc[8 * k : 8 * k + 8, h * LANES : (h + 1) * LANES]


def factor(p, left):
    p = p[...]
    row = lax.broadcasted_iota(jnp.int32, (RANK, 2 * RANK), 0)
    lane = lax.broadcasted_iota(jnp.int32, (RANK, 2 * RANK), 1)
    unit = jnp.where(lane == row + RANK, 1.0, 0.0)
    gram = dot(p, p, ((1,), (1,)), precision=HIGHEST)
    m = jnp.concatenate([gram, unit[:, RANK:]], axis=1)
    for k in range(RANK - 1):
        ratio = m[:, k : k + 1] / m[k : k + 1, k : k + 1]
        m = m - jnp.where(row > k, ratio, 0.0) * m[k : k + 1, :]
    pivot = jnp.sum(jnp.where(lane == row, m, 0.0), axis=1, keepdims=True)
    inverse = m[:, RANK:] / jnp.sqrt(pivot)
    basis = dot(inverse, p, ((1,), (0,)), precision=HIGHEST)
    weight = dot(inverse.T, basis, ((1,), (0,)), precision=HIGHEST) * (1.0 / N_DP)
    t1, t2, t3 = cut(jnp.concatenate([weight.T, inverse], axis=0), 3)
    left[...] = jnp.concatenate([t1, t1, t2, t2, t1, t3], axis=1)


def gathered(x, out):
    size = 4 * TILES
    acc = x[pl.ds(0, size), :]
    for i in range(1, PEERS // 4):
        acc = acc + x[pl.ds(i * size, size), :]
    one = (acc[:TILES] + acc[TILES : 2 * TILES]) + (acc[2 * TILES : 3 * TILES] + acc[3 * TILES :])
    four = jnp.concatenate([one] * 4, axis=0)
    for i in range(PEERS // 4):
        out[pl.ds(i * size, size), :] = four


def finish(raw, left, approx_out, q_out, approx, q_new, sems):
    pending = []
    for i in range(CHUNKS):
        parts = []
        for t in range(i * WIDE // LANES, (i + 1) * WIDE // LANES):
            parts.append(jnp.concatenate([raw[tile_rows(k, t), :] for k in range(RANK // 8)], axis=0))
        r1, r2, r3 = cut(jnp.concatenate(parts, axis=1), 3)
        both = dot(left[...], jnp.concatenate([r1, r2, r1, r2, r3, r1], axis=0), ((1,), (0,)))
        cols = pl.ds(i * WIDE, WIDE)
        approx[:, cols] = both[:ROWS].astype(BF16)
        q_new[:, cols] = both[ROWS:]
        for j, (src, dst) in enumerate(((approx, approx_out), (q_new, q_out))):
            copy = pltpu.make_async_copy(src.at[:, cols], dst.at[:, cols], sems.at[i, j])
            copy.start()
            pending.append(copy)
    for copy in pending:
        copy.wait()


def in_vmem(x):
    return pltpu.with_memory_space_constraint(x, pltpu.VMEM)


def in_hbm(x):
    return pltpu.with_memory_space_constraint(x, pltpu.HBM)


PARAMS = pltpu.CompilerParams(vmem_limit_bytes=LIMIT)
VMEM, HBM = pl.BlockSpec(memory_space=pltpu.VMEM), pl.BlockSpec(memory_space=pltpu.HBM)
CHUNKS = COLS // WIDE
LINEAR = (RANK * TILES, LANES)


def local(grad, error, q_init):
    p, corrected = pl.pallas_call(
        project,
        out_shape=(pltpu.VMEM((RANK, ROWS), F32), pltpu.VMEM((ROWS, COLS), BF16)),
        in_specs=[HBM] * 3,
        out_specs=(VMEM, VMEM),
        scratch_shapes=[
            pltpu.VMEM((ROWS, COLS), BF16),
            pltpu.VMEM((ROWS, COLS), BF16),
            pltpu.VMEM((RANK, COLS), F32),
            pltpu.SemaphoreType.DMA((CHUNKS, 3)),
        ],
        compiler_params=PARAMS,
        name="project",
    )(in_hbm(grad[0, 0]), in_hbm(error[0, 0]), in_hbm(q_init[0].T))
    p = sum_all(p)
    raw = pl.pallas_call(
        partial,
        out_shape=pltpu.VMEM(LINEAR, F32),
        in_specs=[VMEM] * 2,
        out_specs=VMEM,
        compiler_params=PARAMS,
        name="partial",
    )(in_vmem(p), in_vmem(corrected))
    raw = exchange(raw.reshape(PEERS, 1, COLS), ALONG_DP, FIRST_Q)
    left = pl.pallas_call(
        factor,
        out_shape=pltpu.VMEM((ROWS + RANK, 6 * RANK), BF16),
        in_specs=[VMEM],
        out_specs=VMEM,
        compiler_params=PARAMS,
        cost_estimate=pl.CostEstimate(flops=4_000_000_000, bytes_accessed=0, transcendentals=0),
        name="factor",
    )(in_vmem(p))
    raw, left = lax.optimization_barrier((raw, left))
    raw = pl.pallas_call(
        gathered,
        out_shape=pltpu.VMEM(LINEAR, F32),
        in_specs=[VMEM],
        out_specs=VMEM,
        compiler_params=PARAMS,
        name="gathered",
    )(in_vmem(raw.reshape(LINEAR)))
    raw = exchange(raw.reshape(PEERS, 1, COLS), ALONG_DP, FIRST_Q).reshape(LINEAR)
    approx, q_new = pl.pallas_call(
        finish,
        out_shape=(jax.ShapeDtypeStruct((ROWS, COLS), BF16), jax.ShapeDtypeStruct((RANK, COLS), F32)),
        in_specs=[VMEM] * 2,
        out_specs=(HBM, HBM),
        scratch_shapes=[
            pltpu.VMEM((ROWS, COLS), BF16),
            pltpu.VMEM((RANK, COLS), F32),
            pltpu.SemaphoreType.DMA((CHUNKS, 2)),
        ],
        compiler_params=PARAMS,
        name="finish",
    )(in_vmem(raw), in_vmem(left))
    return (approx[None], q_new.T[None])


def solution(mesh):
    placed = (P("dp", None, None, "mp"), P("dp", None, None, "mp"), P(None, "mp", None))
    return jax.shard_map(
        local,
        mesh=mesh,
        in_specs=placed,
        out_specs=(P(None, None, "mp"), P(None, "mp", None)),
        check_vma=False,
    )
```

```python
import jax
import jax.numpy as jnp
import numpy as np
from jax import lax
from jax.experimental import pallas as pl
from jax.experimental.pallas import tpu as pltpu
from jax.sharding import PartitionSpec as P

HIGHEST = lax.Precision.HIGHEST
BOTH = ("dp", "mp")
BITS = ("z2", "z1", "z0", "x1", "x0", "y2", "y1", "y0", "c")
NEAR = ("x1", "x0", "y0", "c")
FAR = ("z2", "z1", "z0", "y2", "y1")
ALONG_DP = ("z2", "z1", "z0", "x1", "x0")
FIRST_P = ("z2", "z1", "x1", "y2", "y0", "c")
FIRST_SCATTER = ('z2', 'z0', 'x1')
FIRST_GATHER = ('z2', 'x1')
ROWS, RANK, COLS, PEERS, N_DP = 256, 32, 2304, 32, 32
LANES = 128
TILES = COLS // LANES
WIDE = 768
LIMIT = 12 * 1024 * 1024
F32, BF16 = jnp.float32, jnp.bfloat16


def places():
    i = np.arange(512)
    return np.stack([i // 64, i // 16 % 4, i // 2 % 8, i % 2], axis=1)


def groups_along(bits, first, far=True):
    ids = np.arange(512).reshape((2,) * 9)
    inner = [i for i, b in enumerate(BITS) if b in bits]
    outer = [i for i, b in enumerate(BITS) if b not in bits]
    groups = np.transpose(ids, outer + inner).reshape(-1, 2 ** len(inner))
    start = sum(1 << (len(BITS) - 1 - i) for i in inner if BITS[i] in first)
    at, size = places(), np.array([8, 4, 8, 2])
    listed = []
    for group in groups:
        root = group[0] ^ start
        apart = np.abs(at[group] - at[root])
        hops = np.minimum(apart, size - apart) @ np.array([4, 4, 4, 1])
        order = np.argsort(-hops if far else hops, kind="stable")
        rest = [int(m) for m in group[order] if m != root]
        listed.append([int(root)] + rest)
    return listed


def exchange(x, bits, first, far=True):
    return lax.all_to_all(x, BOTH, 0, 0, axis_index_groups=groups_along(bits, first, far))


def spread(x, count):
    return jnp.broadcast_to(x[None], (count,) + x.shape)


def sum_all(p):
    near, far = 2 ** len(NEAR), 2 ** len(FAR)
    part = jnp.sum(exchange(p.reshape(near, p.shape[0] // near, p.shape[1]), NEAR, FIRST_P, far=False), axis=0)
    part = jnp.sum(exchange(spread(part, far), FAR, FIRST_P, far=True), axis=0)
    return exchange(spread(part, near), NEAR, FIRST_P, far=False).reshape(p.shape)


def cut(x, count):
    out = []
    for _ in range(count):
        top = x.astype(BF16)
        out.append(top)
        x = x - top.astype(F32)
    return out


def dot(a, b, dims, **kw):
    return lax.dot_general(a, b, (dims, ((), ())), preferred_element_type=F32, **kw)


def project(grad, error, q_init, p_out, corrected, g, e, q, sems):
    def copies(i):
        cols = pl.ds(i * WIDE, WIDE)
        return [
            pltpu.make_async_copy(src.at[:, cols], dst.at[:, cols], sems.at[i, j])
            for j, (src, dst) in enumerate(((grad, g), (error, e), (q_init, q)))
        ]

    for i in range(COLS // WIDE):
        for copy in copies(i):
            copy.start()
    total = jnp.zeros((RANK, ROWS), F32)
    for i in range(COLS // WIDE):
        for copy in copies(i):
            copy.wait()
        cols = pl.ds(i * WIDE, WIDE)
        both = (g[:, cols].astype(F32) + e[:, cols].astype(F32)).astype(BF16)
        corrected[:, cols] = both
        total = total + dot(q[:, cols].astype(BF16), both, ((1,), (1,)))
    p_out[...] = total


def tile_rows(k, t):
    return pl.ds(8 * (k * TILES + t), 8)


def slots():
    scatter = groups_along(ALONG_DP, FIRST_SCATTER, far=True)[0]
    gather = groups_along(ALONG_DP, FIRST_GATHER, far=True)[0]
    return [scatter.index(member) for member in gather]


def partial(p, corrected, out):
    left = jnp.concatenate(cut(p[...], 3), axis=0)
    place = slots()
    for t in range(0, TILES, 2):
        acc = dot(left, corrected[:, pl.ds(t * LANES, 2 * LANES)], ((1,), (0,)))
        acc = acc[:RANK] + acc[RANK : 2 * RANK] + acc[2 * RANK :]
        for h in range(2):
            for k in range(RANK // 8):
                row, end = 8 * (k * TILES + t + h), 8 * (k * TILES + t + h) + 8
                while row < end:
                    chunk, at = divmod(row, TILES)
                    size = min(end - row, TILES - at)
                    first = 8 * k + 8 - (end - row)
                    out[pl.ds(place[chunk] * TILES + at, size), :] = acc[first : first + size, h * LANES : (h + 1) * LANES]
                    row += size


def factor(p, left):
    p = p[...]
    row = lax.broadcasted_iota(jnp.int32, (RANK, 2 * RANK), 0)
    lane = lax.broadcasted_iota(jnp.int32, (RANK, 2 * RANK), 1)
    unit = jnp.where(lane == row + RANK, 1.0, 0.0)
    gram = dot(p, p, ((1,), (1,)), precision=HIGHEST)
    m = jnp.concatenate([gram, unit[:, RANK:]], axis=1)
    for k in range(RANK - 1):
        ratio = m[:, k : k + 1] / m[k : k + 1, k : k + 1]
        m = m - jnp.where(row > k, ratio, 0.0) * m[k : k + 1, :]
    pivot = jnp.sum(jnp.where(lane == row, m, 0.0), axis=1, keepdims=True)
    inverse = m[:, RANK:] / jnp.sqrt(pivot)
    basis = dot(inverse, p, ((1,), (0,)), precision=HIGHEST)
    weight = dot(inverse.T, basis, ((1,), (0,)), precision=HIGHEST) * (1.0 / N_DP)
    t1, t2, t3 = cut(jnp.concatenate([weight.T, inverse], axis=0), 3)
    left[...] = jnp.concatenate([t1, t1, t2, t2, t1, t3], axis=1)


def gathered(x, out):
    size = 4 * TILES
    acc = x[pl.ds(0, size), :]
    for i in range(1, PEERS // 4):
        acc = acc + x[pl.ds(i * size, size), :]
    one = (acc[:TILES] + acc[TILES : 2 * TILES]) + (acc[2 * TILES : 3 * TILES] + acc[3 * TILES :])
    four = jnp.concatenate([one] * 4, axis=0)
    for i in range(PEERS // 4):
        out[pl.ds(i * size, size), :] = four


def finish(raw, left, approx_out, q_out, approx, q_new, sems):
    pending = []
    for i in range(CHUNKS):
        parts = []
        for t in range(i * WIDE // LANES, (i + 1) * WIDE // LANES):
            parts.append(jnp.concatenate([raw[tile_rows(k, t), :] for k in range(RANK // 8)], axis=0))
        r1, r2, r3 = cut(jnp.concatenate(parts, axis=1), 3)
        both = dot(left[...], jnp.concatenate([r1, r2, r1, r2, r3, r1], axis=0), ((1,), (0,)))
        cols = pl.ds(i * WIDE, WIDE)
        approx[:, cols] = both[:ROWS].astype(BF16)
        q_new[:, cols] = both[ROWS:]
        for j, (src, dst) in enumerate(((approx, approx_out), (q_new, q_out))):
            copy = pltpu.make_async_copy(src.at[:, cols], dst.at[:, cols], sems.at[i, j])
            copy.start()
            pending.append(copy)
    for copy in pending:
        copy.wait()


def in_vmem(x):
    return pltpu.with_memory_space_constraint(x, pltpu.VMEM)


def in_hbm(x):
    return pltpu.with_memory_space_constraint(x, pltpu.HBM)


PARAMS = pltpu.CompilerParams(vmem_limit_bytes=LIMIT)
VMEM, HBM = pl.BlockSpec(memory_space=pltpu.VMEM), pl.BlockSpec(memory_space=pltpu.HBM)
CHUNKS = COLS // WIDE
LINEAR = (RANK * TILES, LANES)


def local(grad, error, q_init):
    p, corrected = pl.pallas_call(
        project,
        out_shape=(pltpu.VMEM((RANK, ROWS), F32), pltpu.VMEM((ROWS, COLS), BF16)),
        in_specs=[HBM] * 3,
        out_specs=(VMEM, VMEM),
        scratch_shapes=[
            pltpu.VMEM((ROWS, COLS), BF16),
            pltpu.VMEM((ROWS, COLS), BF16),
            pltpu.VMEM((RANK, COLS), F32),
            pltpu.SemaphoreType.DMA((CHUNKS, 3)),
        ],
        compiler_params=PARAMS,
        name="project",
    )(in_hbm(grad[0, 0]), in_hbm(error[0, 0]), in_hbm(q_init[0].T))
    p = sum_all(p)
    raw = pl.pallas_call(
        partial,
        out_shape=pltpu.VMEM(LINEAR, F32),
        in_specs=[VMEM] * 2,
        out_specs=VMEM,
        compiler_params=PARAMS,
        name="partial",
    )(in_vmem(p), in_vmem(corrected))
    raw = exchange(raw.reshape(PEERS, 1, COLS), ALONG_DP, FIRST_SCATTER, far=True)
    left = pl.pallas_call(
        factor,
        out_shape=pltpu.VMEM((ROWS + RANK, 6 * RANK), BF16),
        in_specs=[VMEM],
        out_specs=VMEM,
        compiler_params=PARAMS,
        cost_estimate=pl.CostEstimate(flops=4_000_000_000, bytes_accessed=0, transcendentals=0),
        name="factor",
    )(in_vmem(p))
    raw, left = lax.optimization_barrier((raw, left))
    raw = pl.pallas_call(
        gathered,
        out_shape=pltpu.VMEM(LINEAR, F32),
        in_specs=[VMEM],
        out_specs=VMEM,
        compiler_params=PARAMS,
        name="gathered",
    )(in_vmem(raw.reshape(LINEAR)))
    raw = exchange(raw.reshape(PEERS, 1, COLS), ALONG_DP, FIRST_GATHER, far=True).reshape(LINEAR)
    approx, q_new = pl.pallas_call(
        finish,
        out_shape=(jax.ShapeDtypeStruct((ROWS, COLS), BF16), jax.ShapeDtypeStruct((RANK, COLS), F32)),
        in_specs=[VMEM] * 2,
        out_specs=(HBM, HBM),
        scratch_shapes=[
            pltpu.VMEM((ROWS, COLS), BF16),
            pltpu.VMEM((RANK, COLS), F32),
            pltpu.SemaphoreType.DMA((CHUNKS, 2)),
        ],
        compiler_params=PARAMS,
        name="finish",
    )(in_vmem(raw), in_vmem(left))
    return (approx[None], q_new.T[None])


def solution(mesh):
    placed = (P("dp", None, None, "mp"), P("dp", None, None, "mp"), P(None, "mp", None))
    return jax.shard_map(
        local,
        mesh=mesh,
        in_specs=placed,
        out_specs=(P(None, None, "mp"), P(None, "mp", None)),
        check_vma=False,
    )
```

```python
import jax
import jax.numpy as jnp
import numpy as np
from jax import lax
from jax.experimental import pallas as pl
from jax.experimental.pallas import tpu as pltpu
from jax.sharding import PartitionSpec as P

HIGHEST = lax.Precision.HIGHEST
BOTH = ("dp", "mp")
BITS = ("z2", "z1", "z0", "x1", "x0", "y2", "y1", "y0", "c")
NEAR = ("x1", "x0", "y0", "c")
FAR = ("z2", "z1", "z0", "y2", "y1")
ALONG_DP = ("z2", "z1", "z0", "x1", "x0")
FIRST_P = ("z2", "z1", "x1", "y2", "y0", "c")
FIRST_SCATTER = ('z2', 'z0', 'x1')
FIRST_GATHER = ('z2', 'x1')
ROWS, RANK, COLS, PEERS, N_DP = 256, 32, 2304, 32, 32
LANES = 128
TILES = COLS // LANES
WIDE = 768
READ = 1152
LIMIT = 12 * 1024 * 1024
F32, BF16 = jnp.float32, jnp.bfloat16


def places():
    i = np.arange(512)
    return np.stack([i // 64, i // 16 % 4, i // 2 % 8, i % 2], axis=1)


def groups_along(bits, first, far=True):
    ids = np.arange(512).reshape((2,) * 9)
    inner = [i for i, b in enumerate(BITS) if b in bits]
    outer = [i for i, b in enumerate(BITS) if b not in bits]
    groups = np.transpose(ids, outer + inner).reshape(-1, 2 ** len(inner))
    start = sum(1 << (len(BITS) - 1 - i) for i in inner if BITS[i] in first)
    at, size = places(), np.array([8, 4, 8, 2])
    listed = []
    for group in groups:
        root = group[0] ^ start
        apart = np.abs(at[group] - at[root])
        hops = np.minimum(apart, size - apart) @ np.array([4, 4, 4, 1])
        order = np.argsort(-hops if far else hops, kind="stable")
        rest = [int(m) for m in group[order] if m != root]
        listed.append([int(root)] + rest)
    return listed


def exchange(x, bits, first, far=True):
    return lax.all_to_all(x, BOTH, 0, 0, axis_index_groups=groups_along(bits, first, far))


def spread(x, count):
    return jnp.broadcast_to(x[None], (count,) + x.shape)


def sum_all(p):
    near, far = 2 ** len(NEAR), 2 ** len(FAR)
    part = jnp.sum(exchange(p.reshape(near, p.shape[0] // near, p.shape[1]), NEAR, FIRST_P, far=False), axis=0)
    part = jnp.sum(exchange(spread(part, far), FAR, FIRST_P, far=True), axis=0)
    return exchange(spread(part, near), NEAR, FIRST_P, far=False).reshape(p.shape)


def cut(x, count):
    out = []
    for _ in range(count):
        top = x.astype(BF16)
        out.append(top)
        x = x - top.astype(F32)
    return out


def dot(a, b, dims, **kw):
    return lax.dot_general(a, b, (dims, ((), ())), preferred_element_type=F32, **kw)


def project(grad, error, q_init, p_out, corrected, g, e, q, sems):
    def copies(i):
        cols = pl.ds(i * READ, READ)
        return [
            pltpu.make_async_copy(src.at[:, cols], dst.at[:, cols], sems.at[i, j])
            for j, (src, dst) in enumerate(((grad, g), (error, e), (q_init, q)))
        ]

    for i in range(COLS // READ):
        for copy in copies(i):
            copy.start()
    total = jnp.zeros((RANK, ROWS), F32)
    for i in range(COLS // READ):
        for copy in copies(i):
            copy.wait()
        cols = pl.ds(i * READ, READ)
        both = (g[:, cols].astype(F32) + e[:, cols].astype(F32)).astype(BF16)
        corrected[:, cols] = both
        total = total + dot(q[:, cols].astype(BF16), both, ((1,), (1,)))
    p_out[...] = total


def tile_rows(k, t):
    return pl.ds(8 * (k * TILES + t), 8)


def slots():
    scatter = groups_along(ALONG_DP, FIRST_SCATTER, far=True)[0]
    gather = groups_along(ALONG_DP, FIRST_GATHER, far=True)[0]
    return [scatter.index(member) for member in gather]


def partial(p, corrected, out):
    left = jnp.concatenate(cut(p[...], 3), axis=0)
    place = slots()
    for t in range(0, TILES, 2):
        acc = dot(left, corrected[:, pl.ds(t * LANES, 2 * LANES)], ((1,), (0,)))
        acc = acc[:RANK] + acc[RANK : 2 * RANK] + acc[2 * RANK :]
        for h in range(2):
            for k in range(RANK // 8):
                row, end = 8 * (k * TILES + t + h), 8 * (k * TILES + t + h) + 8
                while row < end:
                    chunk, at = divmod(row, TILES)
                    size = min(end - row, TILES - at)
                    first = 8 * k + 8 - (end - row)
                    out[pl.ds(place[chunk] * TILES + at, size), :] = acc[first : first + size, h * LANES : (h + 1) * LANES]
                    row += size


def factor(p, left):
    p = p[...]
    row = lax.broadcasted_iota(jnp.int32, (RANK, 2 * RANK), 0)
    lane = lax.broadcasted_iota(jnp.int32, (RANK, 2 * RANK), 1)
    unit = jnp.where(lane == row + RANK, 1.0, 0.0)
    gram = dot(p, p, ((1,), (1,)), precision=HIGHEST)
    m = jnp.concatenate([gram, unit[:, RANK:]], axis=1)
    for k in range(RANK - 1):
        ratio = m[:, k : k + 1] / m[k : k + 1, k : k + 1]
        m = m - jnp.where(row > k, ratio, 0.0) * m[k : k + 1, :]
    pivot = jnp.sum(jnp.where(lane == row, m, 0.0), axis=1, keepdims=True)
    inverse = m[:, RANK:] / jnp.sqrt(pivot)
    basis = dot(inverse, p, ((1,), (0,)), precision=HIGHEST)
    weight = dot(inverse.T, basis, ((1,), (0,)), precision=HIGHEST) * (1.0 / N_DP)
    t1, t2, t3 = cut(jnp.concatenate([weight.T, inverse], axis=0), 3)
    left[...] = jnp.concatenate([t1, t1, t2, t2, t1, t3], axis=1)


def gathered(x, out):
    size = 4 * TILES
    acc = x[pl.ds(0, size), :]
    for i in range(1, PEERS // 4):
        acc = acc + x[pl.ds(i * size, size), :]
    one = (acc[:TILES] + acc[TILES : 2 * TILES]) + (acc[2 * TILES : 3 * TILES] + acc[3 * TILES :])
    four = jnp.concatenate([one] * 4, axis=0)
    for i in range(PEERS // 4):
        out[pl.ds(i * size, size), :] = four


def finish(raw, left, approx_out, q_out, approx, q_new, sems):
    pending = []
    for i in range(CHUNKS):
        parts = []
        for t in range(i * WIDE // LANES, (i + 1) * WIDE // LANES):
            parts.append(jnp.concatenate([raw[tile_rows(k, t), :] for k in range(RANK // 8)], axis=0))
        r1, r2, r3 = cut(jnp.concatenate(parts, axis=1), 3)
        both = dot(left[...], jnp.concatenate([r1, r2, r1, r2, r3, r1], axis=0), ((1,), (0,)))
        cols = pl.ds(i * WIDE, WIDE)
        approx[:, cols] = both[:ROWS].astype(BF16)
        q_new[:, cols] = both[ROWS:]
        for j, (src, dst) in enumerate(((approx, approx_out), (q_new, q_out))):
            copy = pltpu.make_async_copy(src.at[:, cols], dst.at[:, cols], sems.at[i, j])
            copy.start()
            pending.append(copy)
    for copy in pending:
        copy.wait()


def in_vmem(x):
    return pltpu.with_memory_space_constraint(x, pltpu.VMEM)


def in_hbm(x):
    return pltpu.with_memory_space_constraint(x, pltpu.HBM)


PARAMS = pltpu.CompilerParams(vmem_limit_bytes=LIMIT)
VMEM, HBM = pl.BlockSpec(memory_space=pltpu.VMEM), pl.BlockSpec(memory_space=pltpu.HBM)
CHUNKS = COLS // WIDE
LINEAR = (RANK * TILES, LANES)


def local(grad, error, q_init):
    p, corrected = pl.pallas_call(
        project,
        out_shape=(pltpu.VMEM((RANK, ROWS), F32), pltpu.VMEM((ROWS, COLS), BF16)),
        in_specs=[HBM] * 3,
        out_specs=(VMEM, VMEM),
        scratch_shapes=[
            pltpu.VMEM((ROWS, COLS), BF16),
            pltpu.VMEM((ROWS, COLS), BF16),
            pltpu.VMEM((RANK, COLS), F32),
            pltpu.SemaphoreType.DMA((COLS // READ, 3)),
        ],
        compiler_params=PARAMS,
        name="project",
    )(in_hbm(grad[0, 0]), in_hbm(error[0, 0]), in_hbm(q_init[0].T))
    p = sum_all(p)
    raw = pl.pallas_call(
        partial,
        out_shape=pltpu.VMEM(LINEAR, F32),
        in_specs=[VMEM] * 2,
        out_specs=VMEM,
        compiler_params=PARAMS,
        name="partial",
    )(in_vmem(p), in_vmem(corrected))
    raw = exchange(raw.reshape(PEERS, 1, COLS), ALONG_DP, FIRST_SCATTER, far=True)
    left = pl.pallas_call(
        factor,
        out_shape=pltpu.VMEM((ROWS + RANK, 6 * RANK), BF16),
        in_specs=[VMEM],
        out_specs=VMEM,
        compiler_params=PARAMS,
        cost_estimate=pl.CostEstimate(flops=4_000_000_000, bytes_accessed=0, transcendentals=0),
        name="factor",
    )(in_vmem(p))
    raw, left = lax.optimization_barrier((raw, left))
    raw = pl.pallas_call(
        gathered,
        out_shape=pltpu.VMEM(LINEAR, F32),
        in_specs=[VMEM],
        out_specs=VMEM,
        compiler_params=PARAMS,
        name="gathered",
    )(in_vmem(raw.reshape(LINEAR)))
    raw = exchange(raw.reshape(PEERS, 1, COLS), ALONG_DP, FIRST_GATHER, far=True).reshape(LINEAR)
    approx, q_new = pl.pallas_call(
        finish,
        out_shape=(jax.ShapeDtypeStruct((ROWS, COLS), BF16), jax.ShapeDtypeStruct((RANK, COLS), F32)),
        in_specs=[VMEM] * 2,
        out_specs=(HBM, HBM),
        scratch_shapes=[
            pltpu.VMEM((ROWS, COLS), BF16),
            pltpu.VMEM((RANK, COLS), F32),
            pltpu.SemaphoreType.DMA((CHUNKS, 2)),
        ],
        compiler_params=PARAMS,
        name="finish",
    )(in_vmem(raw), in_vmem(left))
    return (approx[None], q_new.T[None])


def solution(mesh):
    placed = (P("dp", None, None, "mp"), P("dp", None, None, "mp"), P(None, "mp", None))
    return jax.shard_map(
        local,
        mesh=mesh,
        in_specs=placed,
        out_specs=(P(None, None, "mp"), P(None, "mp", None)),
        check_vma=False,
    )
```

```python
import jax
import jax.numpy as jnp
import numpy as np
from jax import lax
from jax.experimental import pallas as pl
from jax.experimental.pallas import tpu as pltpu
from jax.sharding import PartitionSpec as P

HIGHEST = lax.Precision.HIGHEST
BOTH = ("dp", "mp")
BITS = ("z2", "z1", "z0", "x1", "x0", "y2", "y1", "y0", "c")
NEAR = ("x1", "x0", "y0", "c")
FAR = ("z2", "z1", "z0", "y2", "y1")
ALONG_DP = ("z2", "z1", "z0", "x1", "x0")
FIRST_P = ("z2", "z1", "x1", "y2", "y0", "c")
FIRST_SCATTER = ('z2', 'z0', 'x1')
FIRST_GATHER = ('z2', 'x1')
ROWS, RANK, COLS, PEERS, N_DP = 256, 32, 2304, 32, 32
LANES = 128
TILES = COLS // LANES
WIDE = 768
LIMIT = 12 * 1024 * 1024
F32, BF16 = jnp.float32, jnp.bfloat16


def places():
    i = np.arange(512)
    return np.stack([i // 64, i // 16 % 4, i // 2 % 8, i % 2], axis=1)


def groups_along(bits, first, far=True):
    ids = np.arange(512).reshape((2,) * 9)
    inner = [i for i, b in enumerate(BITS) if b in bits]
    outer = [i for i, b in enumerate(BITS) if b not in bits]
    groups = np.transpose(ids, outer + inner).reshape(-1, 2 ** len(inner))
    start = sum(1 << (len(BITS) - 1 - i) for i in inner if BITS[i] in first)
    at, size = places(), np.array([8, 4, 8, 2])
    listed = []
    for group in groups:
        root = group[0] ^ start
        apart = np.abs(at[group] - at[root])
        hops = np.minimum(apart, size - apart) @ np.array([4, 4, 4, 1])
        order = np.argsort(-hops if far else hops, kind="stable")
        rest = [int(m) for m in group[order] if m != root]
        listed.append([int(root)] + rest)
    return listed


def exchange(x, bits, first, far=True):
    return lax.all_to_all(x, BOTH, 0, 0, axis_index_groups=groups_along(bits, first, far))


def spread(x, count):
    return jnp.broadcast_to(x[None], (count,) + x.shape)


def sum_all(p):
    near, far = 2 ** len(NEAR), 2 ** len(FAR)
    part = jnp.sum(exchange(p.reshape(near, p.shape[0] // near, p.shape[1]), NEAR, FIRST_P, far=False), axis=0)
    part = jnp.sum(exchange(spread(part, far), FAR, FIRST_P, far=True), axis=0)
    return exchange(spread(part, near), NEAR, FIRST_P, far=False).reshape(p.shape)


def cut(x, count):
    out = []
    for _ in range(count):
        top = x.astype(BF16)
        out.append(top)
        x = x - top.astype(F32)
    return out


def dot(a, b, dims, **kw):
    return lax.dot_general(a, b, (dims, ((), ())), preferred_element_type=F32, **kw)


def project(grad, error, q_init, p_out, corrected, g, e, q, sems):
    def copies(i):
        cols = pl.ds(i * WIDE, WIDE)
        return [
            pltpu.make_async_copy(src.at[:, cols], dst.at[:, cols], sems.at[i, j])
            for j, (src, dst) in enumerate(((grad, g), (error, e), (q_init, q)))
        ]

    for i in range(COLS // WIDE):
        for copy in copies(i):
            copy.start()
    total = jnp.zeros((RANK, ROWS), F32)
    for i in range(COLS // WIDE):
        for copy in copies(i):
            copy.wait()
        cols = pl.ds(i * WIDE, WIDE)
        both = (g[:, cols].astype(F32) + e[:, cols].astype(F32)).astype(BF16)
        corrected[:, cols] = both
        total = total + dot(q[:, cols].astype(BF16), both, ((1,), (1,)))
    p_out[...] = total


def tile_rows(k, t):
    return pl.ds(8 * (k * TILES + t), 8)


def slots():
    scatter = groups_along(ALONG_DP, FIRST_SCATTER, far=True)[0]
    gather = groups_along(ALONG_DP, FIRST_GATHER, far=True)[0]
    return [scatter.index(member) for member in gather]


def partial(p, corrected, out):
    left = jnp.concatenate(cut(p[...], 3), axis=0)
    place = slots()
    for t in range(0, TILES, 2):
        acc = dot(left, corrected[:, pl.ds(t * LANES, 2 * LANES)], ((1,), (0,)))
        acc = acc[:RANK] + acc[RANK : 2 * RANK] + acc[2 * RANK :]
        for h in range(2):
            for k in range(RANK // 8):
                row, end = 8 * (k * TILES + t + h), 8 * (k * TILES + t + h) + 8
                while row < end:
                    chunk, at = divmod(row, TILES)
                    size = min(end - row, TILES - at)
                    first = 8 * k + 8 - (end - row)
                    out[pl.ds(place[chunk] * TILES + at, size), :] = acc[first : first + size, h * LANES : (h + 1) * LANES]
                    row += size


def factor(p, left):
    p = p[...]
    row = lax.broadcasted_iota(jnp.int32, (RANK, 2 * RANK), 0)
    lane = lax.broadcasted_iota(jnp.int32, (RANK, 2 * RANK), 1)
    unit = jnp.where(lane == row + RANK, 1.0, 0.0)
    gram = dot(p, p, ((1,), (1,)), precision=HIGHEST)
    m = jnp.concatenate([gram, unit[:, RANK:]], axis=1)
    for k in range(RANK - 1):
        ratio = m[:, k : k + 1] / m[k : k + 1, k : k + 1]
        m = m - jnp.where(row > k, ratio, 0.0) * m[k : k + 1, :]
    pivot = jnp.sum(jnp.where(lane == row, m, 0.0), axis=1, keepdims=True)
    inverse = m[:, RANK:] / jnp.sqrt(pivot)
    basis = dot(inverse, p, ((1,), (0,)), precision=HIGHEST)
    weight = dot(inverse.T, basis, ((1,), (0,)), precision=HIGHEST) * (1.0 / N_DP)
    t1, t2, t3 = cut(jnp.concatenate([weight.T, inverse], axis=0), 3)
    left[...] = jnp.concatenate([t1, t1, t2, t2, t1, t3], axis=1)


def gathered(x, out):
    size = 4 * TILES
    acc = x[pl.ds(0, size), :]
    for i in range(1, PEERS // 4):
        acc = acc + x[pl.ds(i * size, size), :]
    one = (acc[:TILES] + acc[TILES : 2 * TILES]) + (acc[2 * TILES : 3 * TILES] + acc[3 * TILES :])
    four = jnp.concatenate([one] * 4, axis=0)
    for i in range(PEERS // 4):
        out[pl.ds(i * size, size), :] = four


def finish(raw, left, approx_out, q_out, approx, q_new, sems):
    pending = []
    for i in range(CHUNKS):
        parts = []
        for t in range(i * WIDE // LANES, (i + 1) * WIDE // LANES):
            parts.append(jnp.concatenate([raw[tile_rows(k, t), :] for k in range(RANK // 8)], axis=0))
        r1, r2, r3 = cut(jnp.concatenate(parts, axis=1), 3)
        both = dot(left[...], jnp.concatenate([r1, r2, r1, r2, r3, r1], axis=0), ((1,), (0,)))
        cols = pl.ds(i * WIDE, WIDE)
        approx[:, cols] = both[:ROWS].astype(BF16)
        q_new[:, cols] = both[ROWS:]
        for j, (src, dst) in enumerate(((approx, approx_out), (q_new, q_out))):
            copy = pltpu.make_async_copy(src.at[:, cols], dst.at[:, cols], sems.at[i, j])
            copy.start()
            pending.append(copy)
    for copy in pending:
        copy.wait()


def in_vmem(x):
    return pltpu.with_memory_space_constraint(x, pltpu.VMEM)


def in_hbm(x):
    return pltpu.with_memory_space_constraint(x, pltpu.HBM)


PARAMS = pltpu.CompilerParams(vmem_limit_bytes=LIMIT)
VMEM, HBM = pl.BlockSpec(memory_space=pltpu.VMEM), pl.BlockSpec(memory_space=pltpu.HBM)
CHUNKS = COLS // WIDE
LINEAR = (RANK * TILES, LANES)


def local(grad, error, q_init):
    p, corrected = pl.pallas_call(
        project,
        out_shape=(pltpu.VMEM((RANK, ROWS), F32), pltpu.VMEM((ROWS, COLS), BF16)),
        in_specs=[HBM] * 3,
        out_specs=(VMEM, VMEM),
        scratch_shapes=[
            pltpu.VMEM((ROWS, COLS), BF16),
            pltpu.VMEM((ROWS, COLS), BF16),
            pltpu.VMEM((RANK, COLS), F32),
            pltpu.SemaphoreType.DMA((CHUNKS, 3)),
        ],
        compiler_params=PARAMS,
        name="project",
    )(in_hbm(grad[0, 0]), in_hbm(error[0, 0]), in_hbm(q_init[0].T))
    p = sum_all(p)
    raw = pl.pallas_call(
        partial,
        out_shape=pltpu.VMEM(LINEAR, F32),
        in_specs=[VMEM] * 2,
        out_specs=VMEM,
        compiler_params=PARAMS,
        name="partial",
    )(in_vmem(p), in_vmem(corrected))
    raw = exchange(raw.reshape(PEERS, 1, COLS), ALONG_DP, FIRST_SCATTER, far=True)
    raw, p = lax.optimization_barrier((raw, p))
    left = pl.pallas_call(
        factor,
        out_shape=pltpu.VMEM((ROWS + RANK, 6 * RANK), BF16),
        in_specs=[VMEM],
        out_specs=VMEM,
        compiler_params=PARAMS,
        cost_estimate=pl.CostEstimate(flops=4_000_000_000, bytes_accessed=0, transcendentals=0),
        name="factor",
    )(in_vmem(p))
    raw = pl.pallas_call(
        gathered,
        out_shape=pltpu.VMEM(LINEAR, F32),
        in_specs=[VMEM],
        out_specs=VMEM,
        compiler_params=PARAMS,
        name="gathered",
    )(in_vmem(raw.reshape(LINEAR)))
    raw = exchange(raw.reshape(PEERS, 1, COLS), ALONG_DP, FIRST_GATHER, far=True).reshape(LINEAR)
    approx, q_new = pl.pallas_call(
        finish,
        out_shape=(jax.ShapeDtypeStruct((ROWS, COLS), BF16), jax.ShapeDtypeStruct((RANK, COLS), F32)),
        in_specs=[VMEM] * 2,
        out_specs=(HBM, HBM),
        scratch_shapes=[
            pltpu.VMEM((ROWS, COLS), BF16),
            pltpu.VMEM((RANK, COLS), F32),
            pltpu.SemaphoreType.DMA((CHUNKS, 2)),
        ],
        compiler_params=PARAMS,
        name="finish",
    )(in_vmem(raw), in_vmem(left))
    return (approx[None], q_new.T[None])


def solution(mesh):
    placed = (P("dp", None, None, "mp"), P("dp", None, None, "mp"), P(None, "mp", None))
    return jax.shard_map(
        local,
        mesh=mesh,
        in_specs=placed,
        out_specs=(P(None, None, "mp"), P(None, "mp", None)),
        check_vma=False,
    )
```

```python
import jax
import jax.numpy as jnp
import numpy as np
from jax import lax
from jax.experimental import pallas as pl
from jax.experimental.pallas import tpu as pltpu
from jax.sharding import PartitionSpec as P

HIGHEST = lax.Precision.HIGHEST
BOTH = ("dp", "mp")
BITS = ("z2", "z1", "z0", "x1", "x0", "y2", "y1", "y0", "c")
NEAR = ("x1", "x0", "y0", "c")
FAR = ("z2", "z1", "z0", "y2", "y1")
ALONG_DP = ("z2", "z1", "z0", "x1", "x0")
FIRST_P = ("z2", "z1", "x1", "y2", "y0", "c")
FIRST_SCATTER = ('z2', 'z0', 'x1')
FIRST_GATHER = ('z2', 'x1')
ROWS, RANK, COLS, PEERS, N_DP = 256, 32, 2304, 32, 32
LANES = 128
TILES = COLS // LANES
WIDE = 768
READ = 1152
LIMIT = 12 * 1024 * 1024
F32, BF16 = jnp.float32, jnp.bfloat16


def places():
    i = np.arange(512)
    return np.stack([i // 64, i // 16 % 4, i // 2 % 8, i % 2], axis=1)


def groups_along(bits, first, far=True):
    ids = np.arange(512).reshape((2,) * 9)
    inner = [i for i, b in enumerate(BITS) if b in bits]
    outer = [i for i, b in enumerate(BITS) if b not in bits]
    groups = np.transpose(ids, outer + inner).reshape(-1, 2 ** len(inner))
    start = sum(1 << (len(BITS) - 1 - i) for i in inner if BITS[i] in first)
    at, size = places(), np.array([8, 4, 8, 2])
    listed = []
    for group in groups:
        root = group[0] ^ start
        apart = np.abs(at[group] - at[root])
        hops = np.minimum(apart, size - apart) @ np.array([4, 4, 4, 1])
        order = np.argsort(-hops if far else hops, kind="stable")
        rest = [int(m) for m in group[order] if m != root]
        listed.append([int(root)] + rest)
    return listed


def exchange(x, bits, first, far=True):
    return lax.all_to_all(x, BOTH, 0, 0, axis_index_groups=groups_along(bits, first, far))


def spread(x, count):
    return jnp.broadcast_to(x[None], (count,) + x.shape)


def sum_all(p):
    near, far = 2 ** len(NEAR), 2 ** len(FAR)
    part = jnp.sum(exchange(p.reshape(near, p.shape[0] // near, p.shape[1]), NEAR, FIRST_P, far=False), axis=0)
    part = jnp.sum(exchange(spread(part, far), FAR, FIRST_P, far=True), axis=0)
    return exchange(spread(part, near), NEAR, FIRST_P, far=False).reshape(p.shape)


def cut(x, count):
    out = []
    for _ in range(count):
        top = x.astype(BF16)
        out.append(top)
        x = x - top.astype(F32)
    return out


def dot(a, b, dims, **kw):
    return lax.dot_general(a, b, (dims, ((), ())), preferred_element_type=F32, **kw)


def project(grad, error, q_init, p_out, corrected, g, e, q, sems):
    def copies(i):
        cols = pl.ds(i * READ, READ)
        return [
            pltpu.make_async_copy(src.at[:, cols], dst.at[:, cols], sems.at[i, j])
            for j, (src, dst) in enumerate(((grad, g), (error, e), (q_init, q)))
        ]

    for i in range(COLS // READ):
        for copy in copies(i):
            copy.start()
    total = jnp.zeros((RANK, ROWS), F32)
    for i in range(COLS // READ):
        for copy in copies(i):
            copy.wait()
        cols = pl.ds(i * READ, READ)
        both = (g[:, cols].astype(F32) + e[:, cols].astype(F32)).astype(BF16)
        corrected[:, cols] = both
        total = total + dot(q[:, cols].astype(BF16), both, ((1,), (1,)))
    p_out[...] = total


def tile_rows(k, t):
    return pl.ds(8 * (k * TILES + t), 8)


def slots():
    scatter = groups_along(ALONG_DP, FIRST_SCATTER, far=True)[0]
    gather = groups_along(ALONG_DP, FIRST_GATHER, far=True)[0]
    return [scatter.index(member) for member in gather]


def partial(p, corrected, out):
    left = jnp.concatenate(cut(p[...], 3), axis=0)
    place = slots()
    for t in range(0, TILES, 2):
        acc = dot(left, corrected[:, pl.ds(t * LANES, 2 * LANES)], ((1,), (0,)))
        acc = acc[:RANK] + acc[RANK : 2 * RANK] + acc[2 * RANK :]
        for h in range(2):
            for k in range(RANK // 8):
                row, end = 8 * (k * TILES + t + h), 8 * (k * TILES + t + h) + 8
                while row < end:
                    chunk, at = divmod(row, TILES)
                    size = min(end - row, TILES - at)
                    first = 8 * k + 8 - (end - row)
                    out[pl.ds(place[chunk] * TILES + at, size), :] = acc[first : first + size, h * LANES : (h + 1) * LANES]
                    row += size


def factor(p, left):
    p = p[...]
    row = lax.broadcasted_iota(jnp.int32, (RANK, 2 * RANK), 0)
    lane = lax.broadcasted_iota(jnp.int32, (RANK, 2 * RANK), 1)
    unit = jnp.where(lane == row + RANK, 1.0, 0.0)
    gram = dot(p, p, ((1,), (1,)), precision=HIGHEST)
    m = jnp.concatenate([gram, unit[:, RANK:]], axis=1)
    for k in range(RANK - 1):
        ratio = m[:, k : k + 1] / m[k : k + 1, k : k + 1]
        m = m - jnp.where(row > k, ratio, 0.0) * m[k : k + 1, :]
    pivot = jnp.sum(jnp.where(lane == row, m, 0.0), axis=1, keepdims=True)
    inverse = m[:, RANK:] / jnp.sqrt(pivot)
    basis = dot(inverse, p, ((1,), (0,)), precision=HIGHEST)
    weight = dot(inverse.T, basis, ((1,), (0,)), precision=HIGHEST) * (1.0 / N_DP)
    t1, t2, t3 = cut(jnp.concatenate([weight.T, inverse], axis=0), 3)
    left[...] = jnp.concatenate([t1, t1, t2, t2, t1, t3], axis=1)


def gathered(x, out):
    size = 4 * TILES
    acc = x[pl.ds(0, size), :]
    for i in range(1, PEERS // 4):
        acc = acc + x[pl.ds(i * size, size), :]
    one = (acc[:TILES] + acc[TILES : 2 * TILES]) + (acc[2 * TILES : 3 * TILES] + acc[3 * TILES :])
    four = jnp.concatenate([one] * 4, axis=0)
    for i in range(PEERS // 4):
        out[pl.ds(i * size, size), :] = four


def finish(raw, left, approx_out, q_out, approx, q_new, sems):
    pending = []
    for i in range(CHUNKS):
        parts = []
        for t in range(i * WIDE // LANES, (i + 1) * WIDE // LANES):
            parts.append(jnp.concatenate([raw[tile_rows(k, t), :] for k in range(RANK // 8)], axis=0))
        r1, r2, r3 = cut(jnp.concatenate(parts, axis=1), 3)
        both = dot(left[...], jnp.concatenate([r1, r2, r1, r2, r3, r1], axis=0), ((1,), (0,)))
        cols = pl.ds(i * WIDE, WIDE)
        approx[:, cols] = both[:ROWS].astype(BF16)
        q_new[:, cols] = both[ROWS:]
        for j, (src, dst) in enumerate(((approx, approx_out), (q_new, q_out))):
            copy = pltpu.make_async_copy(src.at[:, cols], dst.at[:, cols], sems.at[i, j])
            copy.start()
            pending.append(copy)
    for copy in pending:
        copy.wait()


def in_vmem(x):
    return pltpu.with_memory_space_constraint(x, pltpu.VMEM)


def in_hbm(x):
    return pltpu.with_memory_space_constraint(x, pltpu.HBM)


PARAMS = pltpu.CompilerParams(vmem_limit_bytes=LIMIT)
VMEM, HBM = pl.BlockSpec(memory_space=pltpu.VMEM), pl.BlockSpec(memory_space=pltpu.HBM)
CHUNKS = COLS // WIDE
LINEAR = (RANK * TILES, LANES)


def local(grad, error, q_init):
    p, corrected = pl.pallas_call(
        project,
        out_shape=(pltpu.VMEM((RANK, ROWS), F32), pltpu.VMEM((ROWS, COLS), BF16)),
        in_specs=[HBM] * 3,
        out_specs=(VMEM, VMEM),
        scratch_shapes=[
            pltpu.VMEM((ROWS, COLS), BF16),
            pltpu.VMEM((ROWS, COLS), BF16),
            pltpu.VMEM((RANK, COLS), F32),
            pltpu.SemaphoreType.DMA((COLS // READ, 3)),
        ],
        compiler_params=PARAMS,
        name="project",
    )(in_hbm(grad[0, 0]), in_hbm(error[0, 0]), in_hbm(q_init[0].T))
    p = sum_all(p)
    raw = pl.pallas_call(
        partial,
        out_shape=pltpu.VMEM(LINEAR, F32),
        in_specs=[VMEM] * 2,
        out_specs=VMEM,
        compiler_params=PARAMS,
        name="partial",
    )(in_vmem(p), in_vmem(corrected))
    raw = exchange(raw.reshape(PEERS, 1, COLS), ALONG_DP, FIRST_SCATTER, far=True)
    raw, p = lax.optimization_barrier((raw, p))
    left = pl.pallas_call(
        factor,
        out_shape=pltpu.VMEM((ROWS + RANK, 6 * RANK), BF16),
        in_specs=[VMEM],
        out_specs=VMEM,
        compiler_params=PARAMS,
        cost_estimate=pl.CostEstimate(flops=4_000_000_000, bytes_accessed=0, transcendentals=0),
        name="factor",
    )(in_vmem(p))
    raw = pl.pallas_call(
        gathered,
        out_shape=pltpu.VMEM(LINEAR, F32),
        in_specs=[VMEM],
        out_specs=VMEM,
        compiler_params=PARAMS,
        name="gathered",
    )(in_vmem(raw.reshape(LINEAR)))
    raw = exchange(raw.reshape(PEERS, 1, COLS), ALONG_DP, FIRST_GATHER, far=True).reshape(LINEAR)
    approx, q_new = pl.pallas_call(
        finish,
        out_shape=(jax.ShapeDtypeStruct((ROWS, COLS), BF16), jax.ShapeDtypeStruct((RANK, COLS), F32)),
        in_specs=[VMEM] * 2,
        out_specs=(HBM, HBM),
        scratch_shapes=[
            pltpu.VMEM((ROWS, COLS), BF16),
            pltpu.VMEM((RANK, COLS), F32),
            pltpu.SemaphoreType.DMA((CHUNKS, 2)),
        ],
        compiler_params=PARAMS,
        name="finish",
    )(in_vmem(raw), in_vmem(left))
    return (approx[None], q_new.T[None])


def solution(mesh):
    placed = (P("dp", None, None, "mp"), P("dp", None, None, "mp"), P(None, "mp", None))
    return jax.shard_map(
        local,
        mesh=mesh,
        in_specs=placed,
        out_specs=(P(None, None, "mp"), P(None, "mp", None)),
        check_vma=False,
    )
```
